512 devices in a mesh: dp: 4 (over x), fsdp: 32 (over z, core), tensor: 4 (over y).
Axes of the slice: x: 4, y: 4, z: 16, core: 2. Of those that a mesh axis runs over, the one named last changes fastest.
Arguments:
- momentum: float32 [4096, 8192], P('fsdp', 'tensor'), may hold values from -60 to 60
- grads: bfloat16 [4, 4096, 8192], P('dp', 'fsdp', 'tensor'), may hold values from -40 to 40
- right_basis: bfloat16 [8192, 512], P('tensor', 'fsdp'), may hold values from -0.0625 to 0.0625
Outputs:
- new_momentum: float32 [4096, 8192], P('fsdp', 'tensor')
- update: bfloat16 [4096, 8192], P('fsdp', 'tensor')
- new_basis: bfloat16 [8192, 512], P('tensor', 'fsdp')
The draws below stay inside these ranges and needn't reach their ends.
All inputs are finite; a program needn't handle non-finite values.
Results may differ from the reference program's by a relative error of at most 0.0016.
Values may be sent and summed in bfloat16 or wider, within the bound.
No kernel may reach another device: no remote copies, remote signals or barrier semaphores. Data moves between devices by JAX's collectives and lax.ppermute only.
A program may use at most 64 MiB of HBM per device.

```python
import math
import jax
import jax.numpy as jnp
from jax import lax

COLS = 8192
RANK = 512
ROWS = 4096
N_DP = 4


def column_scales(key, top):
    position = jnp.arange(COLS, dtype=jnp.float32) / (COLS - 1)
    rough = jnp.exp(jax.random.uniform(key, (COLS,), jnp.float32, 0.0, 0.69))
    return jnp.exp(jnp.log(top) * position) * rough


def draw_momentum(key, part):
    key = jax.random.fold_in(key, 11)
    first, second = jax.random.split(key)
    values = jax.random.truncated_normal(first, -5.0, 5.0, (ROWS, COLS), jnp.float32)
    scales = column_scales(second, 5.0)
    return (values * scales[None, :]).astype(jnp.float32)


def draw_grads(key, part):
    key = jax.random.fold_in(key, 23)
    first, second = jax.random.split(key)
    values = 0.5 * jax.random.truncated_normal(first, -3.5, 3.5, (N_DP, ROWS, COLS), jnp.float32)
    scales = column_scales(second, 5.0)
    return (values * scales[None, None, :]).astype(jnp.bfloat16)


def block_levels(key, shape, cuts, smallest, high):
    loudness = 1.0
    for dim, blocks in cuts:
        steps = jax.random.uniform(jax.random.fold_in(jax.random.fold_in(key, 6), dim), (blocks,), jnp.float32, smallest / len(cuts), high / len(cuts))
        loudness = loudness * jnp.repeat(jnp.exp(steps), shape[dim] // blocks).reshape((-1,) + (1,) * (len(shape) - 1 - dim))
    return loudness


def gaussian(own_key, shape, deviation, bound, cuts=(), held_as=jnp.bfloat16):
    entries = jax.random.normal(own_key, shape, jnp.float32) * deviation
    if len(cuts) > 0:
        entries = block_levels(own_key, shape, cuts, -0.22, 0.18) * entries
    return jnp.clip(entries, min=-bound, max=bound).astype(held_as)


def setup_inputs(seed: int = 0) -> dict:
    arg_keys = jax.random.split(jax.random.key(seed), 4)
    momentum = draw_momentum(jax.random.fold_in(arg_keys[3], 71), 0)
    grads = draw_grads(jax.random.fold_in(arg_keys[3], 71), 0)
    right_basis = gaussian(arg_keys[2], (COLS, RANK), COLS ** -0.5, 0.0625, ((0, 4), (1, 32)))
    return dict(momentum=momentum, grads=grads, right_basis=right_basis)


HIGH = lax.Precision.HIGHEST

def reference(momentum, grads, right_basis):
    total = momentum + lax.optimization_barrier(jnp.sum(grads.astype(jnp.float32), axis=0))
    left = jnp.dot(total, right_basis.astype(jnp.float32), precision=HIGH)
    gram = jnp.dot(left.T, left, precision=HIGH)
    factor = jnp.linalg.cholesky(gram)
    left_basis = jax.scipy.linalg.solve_triangular(factor, left.T, lower=True).T
    right = jnp.dot(total.T, left_basis, precision=HIGH)
    new_momentum = total - 0.05 * jnp.dot(left_basis, right.T, precision=HIGH)
    norms = lax.rsqrt(lax.optimization_barrier(jnp.sum(right * right, axis=0)) + 1e-06)
    scaled = right * norms[None, :]
    new_basis = scaled.astype(jnp.bfloat16)
    factor_scale = math.sqrt(ROWS * COLS / RANK)
    update = (factor_scale * jnp.dot(left_basis, scaled.T, precision=HIGH)).astype(jnp.bfloat16)
    return (new_momentum, update, new_basis)
```

```python
import math

import jax
import jax.numpy as jnp
from jax import lax
from jax.experimental import pallas as pl
from jax.experimental.pallas import tpu as pltpu
from jax.sharding import PartitionSpec as P

HIGH = lax.Precision.HIGHEST
BOTH = ("dp", "tensor")
EDGE = 128


def invert_block(block):
    size = block.shape[0]
    steps = size // 8
    sub = lax.broadcasted_iota(jnp.int32, (8, size), 0)
    lane = lax.broadcasted_iota(jnp.int32, (8, size), 1)
    full = (8, size)
    rows = [block[8 * i : 8 * i + 8] for i in range(steps)]
    done = []
    for k in range(steps):
        here = (lane >= 8 * k) & (lane < 8 * k + 8)
        columns = [[jnp.broadcast_to(r[:, 8 * k + m : 8 * k + m + 1], full) for m in range(8)] for r in rows[k:]]
        cur = jnp.where(here, (lane - 8 * k == sub).astype(jnp.float32), rows[k])
        col = columns[0]
        result = jnp.zeros(full, jnp.float32)
        for j in range(8):
            at = sub == j
            pivot = jnp.broadcast_to(col[j][j : j + 1], full)
            row = jnp.broadcast_to(cur[j : j + 1], full)
            result = jnp.where(at, row * lax.rsqrt(pivot), result)
            recip = 1.0 / pivot
            mult = jnp.where(at, -1.0, col[j])
            cur = jnp.where(at, 0.0, cur) - (mult * row) * recip
            for m in range(j + 1, 8):
                lead = jnp.broadcast_to(col[m][j : j + 1], full)
                col[m] = jnp.where(at, 0.0, col[m]) - (mult * lead) * recip
        done.append(jnp.where(lane <= 8 * k + sub, result, 0.0))
        if k + 1 < steps:
            spread = [jnp.broadcast_to(cur[m : m + 1], full) for m in range(8)]
            for i in range(k + 1, steps):
                acc = jnp.where(here, 0.0, rows[i])
                for m in range(8):
                    acc = acc - columns[i - k][m] * spread[m]
                rows[i] = acc
    return jnp.concatenate(done, axis=0)


def invert_kernel(gram_ref, out_ref, work):
    size = gram_ref.shape[0]
    count = size // EDGE
    work[...] = gram_ref[...]
    out_ref[...] = jnp.zeros_like(out_ref)
    for k in range(count):
        a, b = k * EDGE, (k + 1) * EDGE
        inv = invert_block(work[a:b, a:b])
        if k:
            out_ref[a:b, :a] = jnp.dot(inv, work[a:b, :a], precision=HIGH, preferred_element_type=jnp.float32)
        out_ref[a:b, a:b] = inv
        if b < size:
            upper = jnp.dot(inv, work[a:b, b:], precision=HIGH, preferred_element_type=jnp.float32)
            full = jnp.concatenate([out_ref[a:b, :b], upper], axis=1)
            work[b:, a:b] = jnp.zeros((size - b, EDGE), jnp.float32)
            work[b:, :] -= lax.dot_general(upper, full, (((0,), (0,)), ((), ())), precision=HIGH, preferred_element_type=jnp.float32)


def inverse_factor(gram):
    rank = gram.shape[0]
    return pl.pallas_call(
        invert_kernel,
        out_shape=jax.ShapeDtypeStruct((rank, rank), jnp.float32),
        in_specs=[pl.BlockSpec(memory_space=pltpu.VMEM)],
        out_specs=pl.BlockSpec(memory_space=pltpu.VMEM),
        scratch_shapes=[pltpu.VMEM((rank, rank), jnp.float32)],
        compiler_params=pltpu.CompilerParams(vmem_limit_bytes=16 * 1024 * 1024),
        cost_estimate=pl.CostEstimate(flops=20 * 10**9, bytes_accessed=2 * 4 * rank * rank, transcendentals=0),
        name="inverse_factor",
    )(gram)


def dot(a, b, dims):
    return lax.dot_general(a, b, (dims, ((), ())), precision=HIGH, preferred_element_type=jnp.float32)


def swap(x, axis, groups=None):
    return lax.all_to_all(x, axis, 0, 0, tiled=True, axis_index_groups=groups)


def share(x, n, axis, groups=None):
    return swap(jnp.broadcast_to(x[None], (n,) + x.shape), axis, groups)


def per_device(momentum, grads, right_basis):
    rows, local_cols = momentum.shape
    n_dp, n_fsdp, n_tensor = (lax.axis_size(a) for a in ("dp", "fsdp", "tensor"))
    n_both = n_dp * n_tensor
    n_z = n_fsdp // 2
    near = 4
    far = n_z // near
    rank_local = right_basis.shape[1]
    rank = rank_local * n_fsdp
    cols = local_cols // n_dp
    half = cols // 2
    factor_scale = math.sqrt(rows * n_fsdp * local_cols * n_tensor / rank)
    cores = [[2 * z, 2 * z + 1] for z in range(n_z)]
    zs = [[2 * z + c for z in range(n_z)] for c in range(2)]
    nears = [[2 * (near * h + l) + c for l in range(near)] for h in range(far) for c in range(2)]
    fars = [[2 * (near * h + l) + c for h in range(far)] for l in range(near) for c in range(2)]
    d = lax.axis_index("dp")
    slot = d * n_tensor + lax.axis_index("tensor")
    me = lax.axis_index("fsdp")

    with jax.named_scope("basis"):
        mine = lax.dynamic_slice_in_dim(right_basis.T, d * cols, cols, 1)
        pair = swap(mine.reshape(rank_local, 2, half).transpose(1, 0, 2), "fsdp", cores)
        part = share(pair.reshape(2 * rank_local, half), n_z, "fsdp", zs)
        basis_t = share(part.reshape(rank, half), 2, "fsdp", cores).transpose(1, 0, 2).reshape(rank, cols)
    with jax.named_scope("total"):
        blocks = swap(grads[0].reshape(rows, n_dp, cols).transpose(1, 0, 2), "dp")
        total = lax.dynamic_slice_in_dim(momentum, d * cols, cols, 1) + jnp.sum(blocks.astype(jnp.float32), axis=0)
    with jax.named_scope("left"):
        partial = dot(total, basis_t.astype(jnp.float32), ((1,), (1,)))
        partial = jnp.sum(swap(partial.reshape(n_dp, rows // n_dp, rank), "dp"), axis=0)
        partial = jnp.sum(share(partial, n_tensor, "tensor"), axis=0)
        left = share(partial, n_dp, "dp").reshape(rows, rank)
    with jax.named_scope("product"):
        prod = dot(left, total, ((0,), (0,)))
        prod = jnp.sum(swap(prod.reshape(rank, 2, half).transpose(1, 0, 2), "fsdp", cores), axis=0)
        prod = lax.psum_scatter(prod, "fsdp", scatter_dimension=0, tiled=True, axis_index_groups=zs)
    with jax.named_scope("gram"):
        gram = dot(left, left, ((0,), (0,)))
        gram = lax.dynamic_slice_in_dim(gram, slot * (rank // n_both), rank // n_both, 0)
        gram = jnp.sum(swap(gram.reshape(2, rank // n_both // 2, rank), "fsdp", cores), axis=0)
        gram = jnp.sum(share(gram, near, "fsdp", nears), axis=0)
        gram = jnp.sum(share(gram, far, "fsdp", fars), axis=0)
        gram = share(gram, 2, "fsdp", cores).reshape(rank // n_both, rank)
        gram = share(gram, n_both, BOTH).reshape(rank, rank)
    with jax.named_scope("factor"):
        inverse = inverse_factor(gram)
        prod, inverse = lax.optimization_barrier((prod, inverse))
    with jax.named_scope("right"):
        prod = lax.all_gather(prod, "fsdp", axis=0, tiled=True, axis_index_groups=zs)
        prod = share(prod, 2, "fsdp", cores).transpose(1, 0, 2).reshape(rank, cols)
        left_basis = dot(left, inverse, ((1,), (1,)))
        right_t = dot(inverse, prod, ((1,), (0,)))
    with jax.named_scope("norms"):
        squares = jnp.sum(right_t * right_t, axis=1)
        norms = lax.rsqrt(jnp.sum(share(squares, n_both, BOTH), axis=0) + 1e-06)
        scaled_t = right_t * norms[:, None]
    with jax.named_scope("outputs"):
        new_momentum = total - 0.05 * dot(left_basis, right_t, ((1,), (0,)))
        update = (factor_scale * dot(left_basis, scaled_t, ((1,), (0,)))).astype(jnp.bfloat16)
        basis = lax.dynamic_slice_in_dim(scaled_t, me * rank_local, rank_local, 0).astype(jnp.bfloat16)
        new_momentum = share(new_momentum, n_dp, "dp").transpose(1, 0, 2).reshape(rows, local_cols)
        pack = share(jnp.concatenate([update, basis], axis=0), n_dp, "dp").transpose(1, 0, 2).reshape(rows + rank_local, local_cols)
    return (new_momentum, pack[:rows], pack[rows:].T)


def solution(mesh):
    in_specs = (P("fsdp", "tensor"), P("dp", "fsdp", "tensor"), P("tensor", "fsdp"))
    out_specs = (P("fsdp", "tensor"), P("fsdp", "tensor"), P("tensor", "fsdp"))
    return jax.shard_map(
        per_device, mesh=mesh, in_specs=in_specs, out_specs=out_specs, check_vma=False
    )
```

```python
import functools
import math

import jax
import jax.numpy as jnp
from jax import lax
from jax.experimental import pallas as pl
from jax.experimental.pallas import tpu as pltpu
from jax.sharding import Mesh
from jax.sharding import PartitionSpec as P

HIGH = lax.Precision.HIGHEST
EDGE = 128
VMEM = pl.BlockSpec(memory_space=pltpu.VMEM)
SMEM = pl.BlockSpec(memory_space=pltpu.SMEM)


def dot(a, b, dims):
    return lax.dot_general(a, b, (dims, ((), ())), precision=HIGH, preferred_element_type=jnp.float32)


def call(kernel, shapes, args, flops, scratch=(), scalars=0, dtype=jnp.float32):
    dtypes = dtype if isinstance(dtype, tuple) else (dtype,) * len(shapes)
    return pl.pallas_call(
        kernel,
        out_shape=[jax.ShapeDtypeStruct(s, t) for s, t in zip(shapes, dtypes)],
        in_specs=[SMEM] * scalars + [VMEM] * (len(args) - scalars),
        out_specs=[VMEM] * len(shapes),
        scratch_shapes=[pltpu.VMEM(shape, jnp.float32) for shape in scratch],
        compiler_params=pltpu.CompilerParams(vmem_limit_bytes=32 * 1024 * 1024),
        cost_estimate=pl.CostEstimate(flops=flops, bytes_accessed=4 * 1024 * 1024, transcendentals=0),
        name=kernel.func.__name__ if isinstance(kernel, functools.partial) else kernel.__name__,
    )(*args)


def invert_block(block):
    size = block.shape[0]
    steps = size // 8
    sub = lax.broadcasted_iota(jnp.int32, (8, size), 0)
    lane = lax.broadcasted_iota(jnp.int32, (8, size), 1)
    full = (8, size)
    rows = [block[8 * i : 8 * i + 8] for i in range(steps)]
    done = []
    for k in range(steps):
        here = (lane >= 8 * k) & (lane < 8 * k + 8)
        columns = [[jnp.broadcast_to(r[:, 8 * k + m : 8 * k + m + 1], full) for m in range(8)] for r in rows[k:]]
        cur = jnp.where(here, (lane - 8 * k == sub).astype(jnp.float32), rows[k])
        col = columns[0]
        result = jnp.zeros(full, jnp.float32)
        for j in range(8):
            at = sub == j
            pivot = jnp.broadcast_to(col[j][j : j + 1], full)
            row = jnp.broadcast_to(cur[j : j + 1], full)
            result = jnp.where(at, row * lax.rsqrt(pivot), result)
            recip = 1.0 / pivot
            mult = jnp.where(at, -1.0, col[j])
            cur = jnp.where(at, 0.0, cur) - (mult * row) * recip
            for m in range(j + 1, 8):
                lead = jnp.broadcast_to(col[m][j : j + 1], full)
                col[m] = jnp.where(at, 0.0, col[m]) - (mult * lead) * recip
        done.append(jnp.where(lane <= 8 * k + sub, result, 0.0))
        if k + 1 < steps:
            spread = [jnp.broadcast_to(cur[m : m + 1], full) for m in range(8)]
            for i in range(k + 1, steps):
                acc = jnp.where(here, 0.0, rows[i])
                for m in range(8):
                    acc = acc - columns[i - k][m] * spread[m]
                rows[i] = acc
    return jnp.concatenate(done, axis=0)


def eliminate(work, out, first, last, base):
    size = work.shape[1]
    for k in range(first, last):
        a, b = k * EDGE, (k + 1) * EDGE
        low, high = a - base, b - base
        inv = invert_block(work[low:high, a:b])
        if k:
            out[low:high, :a] = dot(inv, work[low:high, :a], ((1,), (0,)))
        out[low:high, a:b] = inv
        if b < size:
            out[low:high, b:] = jnp.zeros((EDGE, size - b), jnp.float32)
            upper = dot(inv, work[low:high, b:], ((1,), (0,)))
            full = jnp.concatenate([out[low:high, :b], upper], axis=1)
            work[high:, a:b] = jnp.zeros((size - b, EDGE), jnp.float32)
            work[high:, :] -= dot(upper, full, ((0,), (0,)))


def upper_blocks(count):
    return [(k, j) for k in range(count) for j in range(k, count)]


def factor_top(gram_ref, top_ref, rest_ref, work):
    size = work.shape[0]
    count = size // EDGE
    work[...] = jnp.zeros_like(work)
    for at, (k, j) in enumerate(upper_blocks(count)):
        work[k * EDGE : (k + 1) * EDGE, j * EDGE : (j + 1) * EDGE] = gram_ref[at * EDGE : (at + 1) * EDGE, :]
    eliminate(work, top_ref, 0, count // 2, 0)
    rest_ref[...] = work[size // 2 :, :]


def factor_rest(rest_ref, top_ref, left_ref, low_ref, basis_ref, work):
    size = work.shape[1]
    half = size // 2
    count = size // EDGE
    work[...] = rest_ref[...]
    eliminate(work, low_ref, count // 2, count, half)
    basis_ref[:, :half] = dot(left_ref[:, :half], top_ref[:, :half], ((1,), (1,)))
    basis_ref[:, half:] = dot(left_ref[...], low_ref[...], ((1,), (1,)))


def products(near, far, place_ref, left_ref, total_ref, out_ref, gram):
    left = left_ref[...]
    rank = left.shape[1]
    cols = total_ref.shape[1]
    blocks = cols // EDGE
    piece = rank // (2 * near * far)
    prod = dot(left, total_ref[...], ((0,), (0,)))
    for i in range(2 * near * far):
        to, rest = divmod(i, near * far)
        for j in range(blocks):
            at = (rest * blocks + j) * piece
            out_ref[to, at : at + piece, :] = prod[i * piece : (i + 1) * piece, j * EDGE : (j + 1) * EDGE]
    at = 0
    for k in range(rank // EDGE):
        row = dot(left[:, k * EDGE : (k + 1) * EDGE], left[:, k * EDGE :], ((0,), (0,)))
        for j in range(row.shape[1] // EDGE):
            gram[at : at + EDGE, :] = row[:, j * EDGE : (j + 1) * EDGE]
            at += EDGE
    begin = near * far * blocks * piece
    slot = out_ref.shape[1] - begin
    for to in range(2):
        out_ref[to, begin:, :] = gram[pl.ds(pl.multiple_of((2 * place_ref[0] + to) * slot, 8), slot), :]


def finish(prod_ref, top_ref, low_ref, right_ref, squares_ref, prod):
    half = top_ref.shape[0]
    for j in range(prod_ref.shape[1]):
        prod[:, j * EDGE : (j + 1) * EDGE] = prod_ref[:, j].reshape(2 * half, EDGE)
    top = dot(top_ref[:, :half], prod[:half, :], ((1,), (0,)))
    low = dot(low_ref[...], prod[...], ((1,), (0,)))
    right_ref[:half, :] = top
    right_ref[half:, :] = low
    ones = jnp.ones((8, prod.shape[1]), jnp.float32)
    squares_ref[:, :half] = dot(ones, top * top, ((1,), (1,)))
    squares_ref[:, half:] = dot(ones, low * low, ((1,), (1,)))


def outputs(scale, me_ref, squares_ref, basis_ref, right_ref, out_ref):
    rows, rank = basis_ref.shape
    own = out_ref.shape[1] - 2 * rows
    norms = lax.rsqrt(jnp.sum(squares_ref[...], axis=0, keepdims=True) + 1e-06)
    basis = basis_ref[...]
    row = lax.broadcasted_iota(jnp.int32, (own, rank), 0)
    lane = lax.broadcasted_iota(jnp.int32, (own, rank), 1)
    pick = jnp.where(lane == row + me_ref[0] * own, norms, 0.0)
    mixed = dot(jnp.concatenate([0.05 * basis, basis * (scale * norms), pick], axis=0), right_ref[...], ((1,), (0,)))
    mixed = mixed.astype(out_ref.dtype)
    for to in range(out_ref.shape[0]):
        out_ref[to] = mixed


def merge(d_ref, mixed_ref, *refs):
    totals, (momentum_ref, update_ref, basis_ref) = refs[:-3], refs[-3:]
    n = len(totals)
    rows, cols = totals[0].shape
    for k in range(n):
        q = lax.rem(d_ref[0] + (n - k), n)
        at = pl.ds(pl.multiple_of(q * cols, cols), cols)
        momentum_ref[:, at] = totals[k][...] - mixed_ref[q, :rows, :].astype(jnp.float32)
    for q in range(n):
        update_ref[:, q * cols : (q + 1) * cols] = mixed_ref[q, rows : 2 * rows, :]
        basis_ref[:, q * cols : (q + 1) * cols] = mixed_ref[q, 2 * rows :, :]


def swap(x, axis):
    return lax.all_to_all(x, axis, 0, 0, tiled=True)


def share(x, axis):
    return swap(jnp.broadcast_to(x[None], (lax.axis_size(axis),) + x.shape), axis)


def per_device(momentum, grads, right_basis):
    rows, local_cols = momentum.shape
    n_dp, n_far, n_near, n_tensor = (lax.axis_size(a) for a in ("dp", "far", "near", "tensor"))
    n_slots = 2 * n_dp * n_tensor
    rank_local = right_basis.shape[1]
    n_fsdp = 2 * n_far * n_near
    rank = rank_local * n_fsdp
    cols = local_cols // n_dp
    factor_scale = math.sqrt(rows * n_fsdp * local_cols * n_tensor / rank)
    d = lax.axis_index("dp")
    me = lax.axis_index(("far", "near", "core")).reshape(1)
    place = lax.axis_index(("dp", "tensor")).reshape(1)
    slot = len(upper_blocks(rank // EDGE)) * EDGE // n_slots

    def turn(k):
        return [(i, (i + k) % n_dp) for i in range(n_dp)]

    with jax.named_scope("basis"):
        mine = lax.dynamic_slice_in_dim(right_basis.T, d * cols, cols, 1)
        part = share(mine, ("far", "near"))
        basis_t = share(part, "core").transpose(1, 0, 2, 3).reshape(rank, cols)
    with jax.named_scope("total"):
        def column(x, k):
            return lax.dynamic_slice_in_dim(x, (d + k) % n_dp * cols, cols, 1)

        blocks = [lax.ppermute(column(grads[0], k), "dp", turn(k)) for k in range(1, n_dp)]
        total = sum((b.astype(jnp.float32) for b in blocks), column(grads[0], 0).astype(jnp.float32))
        total = column(momentum, 0) + total
    with jax.named_scope("left"):
        partial = dot(total, basis_t.astype(jnp.float32), ((1,), (1,)))
        partial = jnp.sum(swap(partial.reshape(n_dp, rows // n_dp, rank), "dp"), axis=0)
        partial = share(partial, ("dp", "tensor")).reshape(n_dp, n_tensor, rows // n_dp, rank)
        left = jnp.sum(partial, axis=1).reshape(rows, rank)
    with jax.named_scope("totals"):
        totals = [total] + [lax.ppermute(total, "dp", turn(k)) for k in range(1, n_dp)]
    with jax.named_scope("products"):
        prod_rows = rank * cols // EDGE // 2
        both = call(
            functools.partial(products, n_near, n_far),
            [(2, prod_rows + slot, EDGE)],
            (place, left, total),
            10**9,
            [(n_slots * slot, EDGE)],
            1,
        )[0]
        both = jnp.sum(swap(both, "core"), axis=0)
        for axis, n in (("near", n_near), ("far", n_far)):
            prod_rows = both.shape[0] - slot
            prod = both[:prod_rows].reshape(n, prod_rows // n, EDGE)
            gram = jnp.broadcast_to(both[prod_rows:][None], (n, slot, EDGE))
            both = swap(jnp.concatenate([prod, gram], axis=1), axis)
            if axis == "near":
                both, totals[1], totals[3] = lax.optimization_barrier((both, totals[1], totals[3]))
            else:
                both, totals[2] = lax.optimization_barrier((both, totals[2]))
            both = jnp.sum(both, axis=0)
        prod, gram = both[:-slot], both[-slot:]
        gram = share(gram, ("dp", "tensor", "core")).reshape(n_slots * slot, EDGE)
        prod, gram = lax.optimization_barrier((prod, gram))
    with jax.named_scope("factor"):
        half = (rank // 2, rank)
        top, rest = call(factor_top, [half, half], (gram,), 10**10, [(rank, rank)])
        prod = share(prod, "far")
        prod, rest = lax.optimization_barrier((prod, rest))
        low, left_basis = call(factor_rest, [half, (rows, rank)], (rest, top, left), 10**10, [half])
        prod = share(prod, "near")
        prod, low = lax.optimization_barrier((prod, low))
    with jax.named_scope("right"):
        prod = share(prod, "core").reshape(n_fsdp, cols // EDGE, rank_local, EDGE)
        right_t, squares = call(
            finish, [(rank, cols), (8, rank)], (prod, top, low), 2 * 10**9, [(rank, cols)]
        )
    with jax.named_scope("norms"):
        squares = share(squares[:1], ("dp", "tensor")).reshape(n_dp * n_tensor, rank)
    with jax.named_scope("outputs"):
        mixed = call(
            functools.partial(outputs, factor_scale),
            [(n_dp, 2 * rows + rank_local, cols)],
            (me, squares, left_basis, right_t),
            10**9,
            (),
            1,
            jnp.bfloat16,
        )[0]
        mixed = swap(mixed, "dp")
        new_momentum, update, basis = call(
            merge,
            [(rows, local_cols), (rows, local_cols), (rank_local, local_cols)],
            (d.reshape(1), mixed, *totals),
            10**6,
            (),
            1,
            (jnp.float32, jnp.bfloat16, jnp.bfloat16),
        )
    return (new_momentum, update, basis.T)


def solution(mesh):
    n_dp, n_fsdp, n_tensor = (mesh.shape[a] for a in ("dp", "fsdp", "tensor"))
    near = 4
    far = n_fsdp // 2 // near
    fine = Mesh(mesh.devices.reshape(n_dp, far, near, 2, n_tensor), ("dp", "far", "near", "core", "tensor"))
    fsdp = ("far", "near", "core")
    in_specs = (P(fsdp, "tensor"), P("dp", fsdp, "tensor"), P("tensor", fsdp))
    out_specs = (P(fsdp, "tensor"), P(fsdp, "tensor"), P("tensor", fsdp))
    return jax.shard_map(
        per_device, mesh=fine, in_specs=in_specs, out_specs=out_specs, check_vma=False
    )
```

```python
import functools
import math

import jax
import jax.numpy as jnp
from jax import lax
from jax.experimental import pallas as pl
from jax.experimental.pallas import tpu as pltpu
from jax.sharding import Mesh
from jax.sharding import PartitionSpec as P

HIGH = lax.Precision.HIGHEST
EDGE = 128
BOTH = ("dp", "tensor")
VMEM = pl.BlockSpec(memory_space=pltpu.VMEM)
SMEM = pl.BlockSpec(memory_space=pltpu.SMEM)


def dot(a, b, dims):
    return lax.dot_general(a, b, (dims, ((), ())), precision=HIGH, preferred_element_type=jnp.float32)


def call(kernel, shapes, args, flops, scratch=(), scalars=0, dtype=jnp.float32):
    dtypes = dtype if isinstance(dtype, tuple) else (dtype,) * len(shapes)
    return pl.pallas_call(
        kernel,
        out_shape=[jax.ShapeDtypeStruct(s, t) for s, t in zip(shapes, dtypes)],
        in_specs=[SMEM] * scalars + [VMEM] * (len(args) - scalars),
        out_specs=[VMEM] * len(shapes),
        scratch_shapes=[
            pltpu.VMEM(*s) if isinstance(s[-1], type) else pltpu.VMEM(s, jnp.float32) for s in scratch
        ],
        compiler_params=pltpu.CompilerParams(vmem_limit_bytes=32 * 1024 * 1024),
        cost_estimate=pl.CostEstimate(flops=flops, bytes_accessed=4 * 1024 * 1024, transcendentals=0),
        name=kernel.func.__name__ if isinstance(kernel, functools.partial) else kernel.__name__,
    )(*args)


def invert_block(block):
    size = block.shape[0]
    steps = size // 8
    sub = lax.broadcasted_iota(jnp.int32, (8, size), 0)
    lane = lax.broadcasted_iota(jnp.int32, (8, size), 1)
    full = (8, size)
    rows = [block[8 * i : 8 * i + 8] for i in range(steps)]
    done = []
    for k in range(steps):
        here = (lane >= 8 * k) & (lane < 8 * k + 8)
        columns = [[jnp.broadcast_to(r[:, 8 * k + m : 8 * k + m + 1], full) for m in range(8)] for r in rows[k:]]
        cur = jnp.where(here, (lane - 8 * k == sub).astype(jnp.float32), rows[k])
        col = columns[0]
        result = jnp.zeros(full, jnp.float32)
        for j in range(8):
            at = sub == j
            pivot = jnp.broadcast_to(col[j][j : j + 1], full)
            row = jnp.broadcast_to(cur[j : j + 1], full)
            result = jnp.where(at, row * lax.rsqrt(pivot), result)
            recip = 1.0 / pivot
            mult = jnp.where(at, -1.0, col[j])
            cur = jnp.where(at, 0.0, cur) - (mult * row) * recip
            for m in range(j + 1, 8):
                lead = jnp.broadcast_to(col[m][j : j + 1], full)
                col[m] = jnp.where(at, 0.0, col[m]) - (mult * lead) * recip
        done.append(jnp.where(lane <= 8 * k + sub, result, 0.0))
        if k + 1 < steps:
            spread = [jnp.broadcast_to(cur[m : m + 1], full) for m in range(8)]
            for i in range(k + 1, steps):
                acc = jnp.where(here, 0.0, rows[i])
                for m in range(8):
                    acc = acc - columns[i - k][m] * spread[m]
                rows[i] = acc
    return jnp.concatenate(done, axis=0)


def eliminate(work, out, first, last, base):
    size = work.shape[1]
    for k in range(first, last):
        a, b = k * EDGE, (k + 1) * EDGE
        low, high = a - base, b - base
        inv = invert_block(work[low:high, a:b])
        if k:
            out[low:high, :a] = dot(inv, work[low:high, :a], ((1,), (0,)))
        out[low:high, a:b] = inv
        if b < size:
            out[low:high, b:] = jnp.zeros((EDGE, size - b), jnp.float32)
            upper = dot(inv, work[low:high, b:], ((1,), (0,)))
            full = jnp.concatenate([out[low:high, :b], upper], axis=1)
            work[high:, a:b] = jnp.zeros((size - b, EDGE), jnp.float32)
            work[high:, :] -= dot(upper, full, ((0,), (0,)))


def upper_blocks(count):
    return [(k, j) for k in range(count) for j in range(k, count)]


def factor_top(core_ref, own_ref, other_ref, top_ref, rest_ref, work, gram):
    size = work.shape[0]
    count = size // EDGE
    slot = own_ref.shape[1]
    for refs, core in ((own_ref, core_ref[0]), (other_ref, 1 - core_ref[0])):
        for j in range(refs.shape[0]):
            gram[pl.ds(pl.multiple_of((2 * j + core) * slot, 8), slot), :] = refs[j]
    work[...] = jnp.zeros_like(work)
    for at, (k, j) in enumerate(upper_blocks(count)):
        work[k * EDGE : (k + 1) * EDGE, j * EDGE : (j + 1) * EDGE] = gram[at * EDGE : (at + 1) * EDGE, :]
    eliminate(work, top_ref, 0, count // 2, 0)
    rest_ref[...] = work[size // 2 :, :]


def factor_rest(rest_ref, top_ref, left_ref, low_ref, basis_ref, work):
    size = work.shape[1]
    half = size // 2
    count = size // EDGE
    work[...] = rest_ref[...]
    eliminate(work, low_ref, count // 2, count, half)
    basis_ref[:, :half] = dot(left_ref[:, :half], top_ref[:, :half], ((1,), (1,)))
    basis_ref[:, half:] = dot(left_ref[...], low_ref[...], ((1,), (1,)))


def left_part(core_ref, own_ref, other_ref, total_ref, out_ref, basis):
    count, ranks, _ = own_ref.shape
    for refs, core in ((own_ref, core_ref[0]), (other_ref, 1 - core_ref[0])):
        for z in range(count):
            basis[pl.ds(pl.multiple_of((2 * z + core) * ranks, ranks), ranks), :] = refs[z]
    rest = total_ref[...]
    left = jnp.zeros(out_ref.shape, jnp.float32)
    for _ in range(3):
        part = rest.astype(jnp.bfloat16)
        left += lax.dot_general(part, basis[...], (((1,), (1,)), ((), ())), preferred_element_type=jnp.float32)
        rest -= part.astype(jnp.float32)
    out_ref[...] = left


def products(near, far, place_ref, core_ref, left_ref, total_ref, keep_ref, send_ref, out, gram):
    left = left_ref[...]
    rank = left.shape[1]
    cols = total_ref.shape[1]
    blocks = cols // EDGE
    piece = rank // (2 * near * far)
    prod = dot(left, total_ref[...], ((0,), (0,)))
    for i in range(2 * near * far):
        to, rest = divmod(i, near * far)
        for j in range(blocks):
            at = (rest * blocks + j) * piece
            out[to, at : at + piece, :] = prod[i * piece : (i + 1) * piece, j * EDGE : (j + 1) * EDGE]
    at = 0
    for k in range(rank // EDGE):
        row = dot(left[:, k * EDGE : (k + 1) * EDGE], left[:, k * EDGE :], ((0,), (0,)))
        for j in range(row.shape[1] // EDGE):
            gram[at : at + EDGE, :] = row[:, j * EDGE : (j + 1) * EDGE]
            at += EDGE
    begin = near * far * blocks * piece
    slot = out.shape[1] - begin
    for to in range(2):
        out[to, begin:, :] = gram[pl.ds(pl.multiple_of((2 * place_ref[0] + to) * slot, 8), slot), :]
    keep_ref[...] = out[core_ref[0]]
    send_ref[...] = out[1 - core_ref[0]]


def finish(core_ref, own_ref, other_ref, top_ref, low_ref, right_ref, squares_ref, prod):
    half = top_ref.shape[0]
    for refs, core in ((own_ref, core_ref[0]), (other_ref, 1 - core_ref[0])):
        at = pl.ds(pl.multiple_of(core * half, half), half)
        for j in range(refs.shape[1]):
            prod[at, j * EDGE : (j + 1) * EDGE] = refs[:, j].reshape(half, EDGE)
    top = dot(top_ref[:, :half], prod[:half, :], ((1,), (0,)))
    low = dot(low_ref[...], prod[...], ((1,), (0,)))
    right_ref[:half, :] = top
    right_ref[half:, :] = low
    ones = jnp.ones((8, prod.shape[1]), jnp.float32)
    squares_ref[:, :half] = dot(ones, top * top, ((1,), (1,)))
    squares_ref[:, half:] = dot(ones, low * low, ((1,), (1,)))


def outputs(scale, me_ref, squares_ref, basis_ref, right_ref, out_ref):
    rows, rank = basis_ref.shape
    own = out_ref.shape[1] - 2 * rows
    norms = lax.rsqrt(jnp.sum(squares_ref[...], axis=0, keepdims=True) + 1e-06)
    basis = basis_ref[...]
    row = lax.broadcasted_iota(jnp.int32, (own, rank), 0)
    lane = lax.broadcasted_iota(jnp.int32, (own, rank), 1)
    pick = jnp.where(lane == row + me_ref[0] * own, norms, 0.0)
    mixed = dot(jnp.concatenate([0.05 * basis, basis * (scale * norms), pick], axis=0), right_ref[...], ((1,), (0,)))
    mixed = mixed.astype(out_ref.dtype)
    for to in range(out_ref.shape[0]):
        out_ref[to] = mixed


def merge(d_ref, mixed_ref, *refs):
    totals, (momentum_ref, update_ref, basis_ref) = refs[:-3], refs[-3:]
    n = len(totals)
    rows, cols = totals[0].shape
    for k in range(n):
        q = lax.rem(d_ref[0] + (n - k), n)
        at = pl.ds(pl.multiple_of(q * cols, cols), cols)
        momentum_ref[:, at] = totals[k][...] - mixed_ref[q, :rows, :].astype(jnp.float32)
    for q in range(n):
        update_ref[:, q * cols : (q + 1) * cols] = mixed_ref[q, rows : 2 * rows, :]
        basis_ref[:, q * cols : (q + 1) * cols] = mixed_ref[q, 2 * rows :, :]


def swap(x, axis):
    return lax.all_to_all(x, axis, 0, 0, tiled=True)


def share(x, axis):
    return swap(jnp.broadcast_to(x[None], (lax.axis_size(axis),) + x.shape), axis)


def other_core(x):
    return lax.ppermute(x, "core", [(0, 1), (1, 0)])


def per_device(momentum, grads, right_basis):
    rows, local_cols = momentum.shape
    n_dp, n_far, n_near, n_tensor = (lax.axis_size(a) for a in ("dp", "far", "near", "tensor"))
    n_slots = 2 * n_dp * n_tensor
    rank_local = right_basis.shape[1]
    n_fsdp = 2 * n_far * n_near
    rank = rank_local * n_fsdp
    cols = local_cols // n_dp
    factor_scale = math.sqrt(rows * n_fsdp * local_cols * n_tensor / rank)
    d = lax.axis_index("dp")
    me = lax.axis_index(("far", "near", "core")).reshape(1)
    place = lax.axis_index(BOTH).reshape(1)
    core = lax.axis_index("core").reshape(1)
    slot = len(upper_blocks(rank // EDGE)) * EDGE // n_slots

    def turn(k):
        return [(i, (i + k) % n_dp) for i in range(n_dp)]

    with jax.named_scope("basis"):
        mine = lax.dynamic_slice_in_dim(right_basis.T, d * cols, cols, 1)
        part = share(mine, ("far", "near"))
        other = other_core(part)
    with jax.named_scope("total"):
        def column(x, k):
            return lax.dynamic_slice_in_dim(x, (d + k) % n_dp * cols, cols, 1)

        blocks = [lax.ppermute(column(grads[0], k), "dp", turn(k)) for k in range(1, n_dp)]
        total = sum((b.astype(jnp.float32) for b in blocks), column(grads[0], 0).astype(jnp.float32))
        total = column(momentum, 0) + total
    with jax.named_scope("left"):
        partial = call(left_part, [(rows, rank)], (core, part, other, total), 10**9, [((rank, cols), jnp.bfloat16)], 1)[0]
        partial = swap(partial.reshape(n_dp * n_tensor, rows // (n_dp * n_tensor), rank), BOTH)
        left = share(jnp.sum(partial, axis=0), BOTH).reshape(rows, rank)
    with jax.named_scope("totals"):
        totals = [total] + [lax.ppermute(total, "dp", turn(k)) for k in range(1, n_dp)]
    with jax.named_scope("products"):
        prod_rows = rank * cols // EDGE // 2
        keep, send = call(
            functools.partial(products, n_near, n_far),
            [(prod_rows + slot, EDGE)] * 2,
            (place, core, left, total),
            10**9,
            [(2, prod_rows + slot, EDGE), (n_slots * slot, EDGE)],
            2,
        )
        both = keep + other_core(send)
        for axis, n in (("near", n_near), ("far", n_far)):
            prod_rows = both.shape[0] - slot
            prod = both[:prod_rows].reshape(n, prod_rows // n, EDGE)
            gram = jnp.broadcast_to(both[prod_rows:][None], (n, slot, EDGE))
            both = swap(jnp.concatenate([prod, gram], axis=1), axis)
            if axis == "near":
                both, totals[1], totals[3] = lax.optimization_barrier((both, totals[1], totals[3]))
            else:
                both, totals[2] = lax.optimization_barrier((both, totals[2]))
            both = jnp.sum(both, axis=0)
        prod, gram = both[:-slot], both[-slot:]
        gram = share(gram, BOTH)
        prod, gram = lax.optimization_barrier((prod, gram))
    with jax.named_scope("factor"):
        half = (rank // 2, rank)
        top, rest = call(
            factor_top,
            [half, half],
            (core, gram, other_core(gram)),
            10**10,
            [(rank, rank), (n_slots * slot, EDGE)],
            1,
        )
        prod = share(prod, "far")
        prod, rest = lax.optimization_barrier((prod, rest))
        low, left_basis = call(factor_rest, [half, (rows, rank)], (rest, top, left), 10**10, [half])
        prod = share(prod, "near")
        prod, low = lax.optimization_barrier((prod, low))
    with jax.named_scope("right"):
        prod = prod.reshape(n_fsdp // 2, cols // EDGE, rank_local, EDGE)
        right_t, squares = call(
            finish,
            [(rank, cols), (8, rank)],
            (core, prod, other_core(prod), top, low),
            2 * 10**9,
            [(rank, cols)],
            1,
        )
    with jax.named_scope("norms"):
        squares = share(squares[:1], BOTH).reshape(n_dp * n_tensor, rank)
    with jax.named_scope("outputs"):
        mixed = call(
            functools.partial(outputs, factor_scale),
            [(n_dp, 2 * rows + rank_local, cols)],
            (me, squares, left_basis, right_t),
            10**9,
            (),
            1,
            jnp.bfloat16,
        )[0]
        mixed = swap(mixed, "dp")
        new_momentum, update, basis = call(
            merge,
            [(rows, local_cols), (rows, local_cols), (rank_local, local_cols)],
            (d.reshape(1), mixed, *totals),
            10**6,
            (),
            1,
            (jnp.float32, jnp.bfloat16, jnp.bfloat16),
        )
    return (new_momentum, update, basis.T)


def solution(mesh):
    n_dp, n_fsdp, n_tensor = (mesh.shape[a] for a in ("dp", "fsdp", "tensor"))
    near = 4
    far = n_fsdp // 2 // near
    fine = Mesh(mesh.devices.reshape(n_dp, far, near, 2, n_tensor), ("dp", "far", "near", "core", "tensor"))
    fsdp = ("far", "near", "core")
    in_specs = (P(fsdp, "tensor"), P("dp", fsdp, "tensor"), P("tensor", fsdp))
    out_specs = (P(fsdp, "tensor"), P(fsdp, "tensor"), P("tensor", fsdp))
    return jax.shard_map(
        per_device, mesh=fine, in_specs=in_specs, out_specs=out_specs, check_vma=False
    )
```

```python
import functools
import math

import jax
import jax.numpy as jnp
from jax import lax
from jax.experimental import pallas as pl
from jax.experimental.pallas import tpu as pltpu
from jax.sharding import Mesh
from jax.sharding import PartitionSpec as P

HIGH = lax.Precision.HIGHEST
EDGE = 128
BOTH = ("dp", "tensor")
VMEM = pl.BlockSpec(memory_space=pltpu.VMEM)
SMEM = pl.BlockSpec(memory_space=pltpu.SMEM)


def dot(a, b, dims):
    return lax.dot_general(a, b, (dims, ((), ())), precision=HIGH, preferred_element_type=jnp.float32)


def call(kernel, shapes, args, flops, scratch=(), scalars=0, dtype=jnp.float32):
    dtypes = dtype if isinstance(dtype, tuple) else (dtype,) * len(shapes)
    return pl.pallas_call(
        kernel,
        out_shape=[jax.ShapeDtypeStruct(s, t) for s, t in zip(shapes, dtypes)],
        in_specs=[SMEM] * scalars + [VMEM] * (len(args) - scalars),
        out_specs=[VMEM] * len(shapes),
        scratch_shapes=[
            pltpu.VMEM(*s) if isinstance(s[-1], type) else pltpu.VMEM(s, jnp.float32) for s in scratch
        ],
        compiler_params=pltpu.CompilerParams(vmem_limit_bytes=32 * 1024 * 1024),
        cost_estimate=pl.CostEstimate(flops=flops, bytes_accessed=4 * 1024 * 1024, transcendentals=0),
        name=kernel.func.__name__ if isinstance(kernel, functools.partial) else kernel.__name__,
    )(*args)


def invert_block(block):
    size = block.shape[0]
    steps = size // 8
    sub = lax.broadcasted_iota(jnp.int32, (8, size), 0)
    lane = lax.broadcasted_iota(jnp.int32, (8, size), 1)
    full = (8, size)
    rows = [block[8 * i : 8 * i + 8] for i in range(steps)]
    done = []
    for k in range(steps):
        here = (lane >= 8 * k) & (lane < 8 * k + 8)
        columns = [[jnp.broadcast_to(r[:, 8 * k + m : 8 * k + m + 1], full) for m in range(8)] for r in rows[k:]]
        cur = jnp.where(here, (lane - 8 * k == sub).astype(jnp.float32), rows[k])
        col = columns[0]
        result = jnp.zeros(full, jnp.float32)
        for j in range(8):
            at = sub == j
            pivot = jnp.broadcast_to(col[j][j : j + 1], full)
            row = jnp.broadcast_to(cur[j : j + 1], full)
            result = jnp.where(at, row * lax.rsqrt(pivot), result)
            recip = 1.0 / pivot
            mult = jnp.where(at, -1.0, col[j])
            cur = jnp.where(at, 0.0, cur) - (mult * row) * recip
            for m in range(j + 1, 8):
                lead = jnp.broadcast_to(col[m][j : j + 1], full)
                col[m] = jnp.where(at, 0.0, col[m]) - (mult * lead) * recip
        done.append(jnp.where(lane <= 8 * k + sub, result, 0.0))
        if k + 1 < steps:
            spread = [jnp.broadcast_to(cur[m : m + 1], full) for m in range(8)]
            for i in range(k + 1, steps):
                acc = jnp.where(here, 0.0, rows[i])
                for m in range(8):
                    acc = acc - columns[i - k][m] * spread[m]
                rows[i] = acc
    return jnp.concatenate(done, axis=0)


def upper_blocks(count):
    return [(k, j) for k in range(count) for j in range(k, count)]


def factor_top(core_ref, own_ref, other_ref, top_ref, gram):
    slot = own_ref.shape[1]
    for refs, core in ((own_ref, core_ref[0]), (other_ref, 1 - core_ref[0])):
        for j in range(refs.shape[0]):
            gram[pl.ds(pl.multiple_of((2 * j + core) * slot, 8), slot), :] = refs[j]
    g00, g01, g02, g03, g11, g12, g13, g22, g23, g33 = (
        gram[at * EDGE : (at + 1) * EDGE, :] for at in range(len(upper_blocks(4)))
    )
    e1, e2, e3 = EDGE, 2 * EDGE, 3 * EDGE
    inv = invert_block(g00)
    upper = dot(inv, jnp.concatenate([g01, g02, g03], axis=1), ((1,), (0,)))
    top_ref[:e1, :e1] = inv
    top_ref[:e1, e1:e2] = jnp.zeros((e1, e1), jnp.float32)
    top_ref[:e1, e2:] = upper[:, e1:]
    less = dot(upper[:, :e1], jnp.concatenate([inv, upper], axis=1), ((0,), (0,)))
    inv = invert_block(g11 - less[:, e1:e2])
    top_ref[e1:e2, :e1] = dot(inv, -less[:, :e1], ((1,), (0,)))
    top_ref[e1:e2, e1:e2] = inv
    top_ref[e1:e2, e2:] = dot(inv, jnp.concatenate([g12, g13], axis=1) - less[:, e2:], ((1,), (0,)))
    top_ref[e2:, :] = jnp.concatenate([g22, g23, g33, jnp.zeros_like(g33)], axis=1)


def factor_rest(top_ref, left_ref, low_ref, basis_ref):
    e1, e2, e3 = EDGE, 2 * EDGE, 3 * EDGE
    less = dot(top_ref[:e2, e2:], top_ref[:e2, :], ((0,), (0,)))
    inv = invert_block(top_ref[e2:, :e1] - less[:e1, e2:e3])
    upper = dot(inv, top_ref[e2:, e1:e2] - less[:e1, e3:], ((1,), (0,)))
    row = dot(inv, -less[:e1, :e2], ((1,), (0,)))
    low_ref[:e1, :e2] = row
    low_ref[:e1, e2:e3] = inv
    low_ref[:e1, e3:] = jnp.zeros((e1, e1), jnp.float32)
    last = dot(upper, jnp.concatenate([row, inv, upper], axis=1), ((0,), (0,)))
    inv = invert_block(top_ref[e2:, e2:e3] - less[e1:, e3:] - last[:, e3:])
    row = jnp.concatenate([-less[e1:, :e2] - last[:, :e2], -last[:, e2:e3]], axis=1)
    low_ref[e1:, :e3] = dot(inv, row, ((1,), (0,)))
    low_ref[e1:, e3:] = inv
    basis_ref[:, :e2] = dot(left_ref[:, :e2], top_ref[:e2, :e2], ((1,), (1,)))
    basis_ref[:, e2:] = dot(left_ref[...], low_ref[...], ((1,), (1,)))


def left_part(core_ref, own_ref, other_ref, total_ref, out_ref, basis):
    count, ranks, _ = own_ref.shape
    for refs, core in ((own_ref, core_ref[0]), (other_ref, 1 - core_ref[0])):
        for z in range(count):
            basis[pl.ds(pl.multiple_of((2 * z + core) * ranks, ranks), ranks), :] = refs[z]
    rest = total_ref[...]
    left = jnp.zeros(out_ref.shape, jnp.float32)
    for _ in range(3):
        part = rest.astype(jnp.bfloat16)
        left += lax.dot_general(part, basis[...], (((1,), (1,)), ((), ())), preferred_element_type=jnp.float32)
        rest -= part.astype(jnp.float32)
    out_ref[...] = left


def products(near, far, place_ref, core_ref, left_ref, total_ref, keep_ref, send_ref, out, gram):
    left = left_ref[...]
    rank = left.shape[1]
    cols = total_ref.shape[1]
    blocks = cols // EDGE
    piece = rank // (2 * near * far)
    prod = dot(left, total_ref[...], ((0,), (0,)))
    for i in range(2 * near * far):
        to, rest = divmod(i, near * far)
        for j in range(blocks):
            at = (rest * blocks + j) * piece
            out[to, at : at + piece, :] = prod[i * piece : (i + 1) * piece, j * EDGE : (j + 1) * EDGE]
    at = 0
    for k in range(rank // EDGE):
        row = dot(left[:, k * EDGE : (k + 1) * EDGE], left[:, k * EDGE :], ((0,), (0,)))
        for j in range(row.shape[1] // EDGE):
            gram[at : at + EDGE, :] = row[:, j * EDGE : (j + 1) * EDGE]
            at += EDGE
    begin = near * far * blocks * piece
    slot = out.shape[1] - begin
    for to in range(2):
        out[to, begin:, :] = gram[pl.ds(pl.multiple_of((2 * place_ref[0] + to) * slot, 8), slot), :]
    keep_ref[...] = out[core_ref[0]]
    send_ref[...] = out[1 - core_ref[0]]


def finish(core_ref, own_ref, other_ref, top_ref, low_ref, right_ref, squares_ref, prod):
    half = low_ref.shape[0]
    for refs, core in ((own_ref, core_ref[0]), (other_ref, 1 - core_ref[0])):
        at = pl.ds(pl.multiple_of(core * half, half), half)
        for j in range(refs.shape[1]):
            prod[at, j * EDGE : (j + 1) * EDGE] = refs[:, j].reshape(half, EDGE)
    top = dot(top_ref[:half, :half], prod[:half, :], ((1,), (0,)))
    low = dot(low_ref[...], prod[...], ((1,), (0,)))
    right_ref[:half, :] = top
    right_ref[half:, :] = low
    ones = jnp.ones((8, prod.shape[1]), jnp.float32)
    squares_ref[:, :half] = dot(ones, top * top, ((1,), (1,)))
    squares_ref[:, half:] = dot(ones, low * low, ((1,), (1,)))


def outputs(scale, me_ref, squares_ref, basis_ref, right_ref, out_ref):
    rows, rank = basis_ref.shape
    own = out_ref.shape[1] - 2 * rows
    norms = lax.rsqrt(jnp.sum(squares_ref[...], axis=0, keepdims=True) + 1e-06)
    basis = basis_ref[...]
    row = lax.broadcasted_iota(jnp.int32, (own, rank), 0)
    lane = lax.broadcasted_iota(jnp.int32, (own, rank), 1)
    pick = jnp.where(lane == row + me_ref[0] * own, norms, 0.0)
    mixed = dot(jnp.concatenate([0.05 * basis, basis * (scale * norms), pick], axis=0), right_ref[...], ((1,), (0,)))
    mixed = mixed.astype(out_ref.dtype)
    for to in range(out_ref.shape[0]):
        out_ref[to] = mixed


def merge(d_ref, mixed_ref, *refs):
    totals, (momentum_ref, update_ref, basis_ref) = refs[:-3], refs[-3:]
    n = len(totals)
    rows, cols = totals[0].shape
    for k in range(n):
        q = lax.rem(d_ref[0] + (n - k), n)
        at = pl.ds(pl.multiple_of(q * cols, cols), cols)
        momentum_ref[:, at] = totals[k][...] - mixed_ref[q, :rows, :].astype(jnp.float32)
    for q in range(n):
        update_ref[:, q * cols : (q + 1) * cols] = mixed_ref[q, rows : 2 * rows, :]
        basis_ref[:, q * cols : (q + 1) * cols] = mixed_ref[q, 2 * rows :, :]


def swap(x, axis):
    return lax.all_to_all(x, axis, 0, 0, tiled=True)


def share(x, axis):
    return swap(jnp.broadcast_to(x[None], (lax.axis_size(axis),) + x.shape), axis)


def other_core(x):
    return lax.ppermute(x, "core", [(0, 1), (1, 0)])


def per_device(momentum, grads, right_basis):
    rows, local_cols = momentum.shape
    n_dp, n_far, n_near, n_tensor = (lax.axis_size(a) for a in ("dp", "far", "near", "tensor"))
    n_slots = 2 * n_dp * n_tensor
    rank_local = right_basis.shape[1]
    n_fsdp = 2 * n_far * n_near
    rank = rank_local * n_fsdp
    cols = local_cols // n_dp
    factor_scale = math.sqrt(rows * n_fsdp * local_cols * n_tensor / rank)
    d = lax.axis_index("dp")
    me = lax.axis_index(("far", "near", "core")).reshape(1)
    place = lax.axis_index(BOTH).reshape(1)
    core = lax.axis_index("core").reshape(1)
    slot = len(upper_blocks(rank // EDGE)) * EDGE // n_slots

    def turn(k):
        return [(i, (i + k) % n_dp) for i in range(n_dp)]

    with jax.named_scope("basis"):
        mine = lax.dynamic_slice_in_dim(right_basis.T, d * cols, cols, 1)
        part = share(mine, ("far", "near"))
        other = other_core(part)
    with jax.named_scope("total"):
        def column(x, k):
            return lax.dynamic_slice_in_dim(x, (d + k) % n_dp * cols, cols, 1)

        blocks = [lax.ppermute(column(grads[0], k), "dp", turn(k)) for k in range(1, n_dp)]
        total = sum((b.astype(jnp.float32) for b in blocks), column(grads[0], 0).astype(jnp.float32))
        total = column(momentum, 0) + total
    with jax.named_scope("left"):
        partial = call(left_part, [(rows, rank)], (core, part, other, total), 10**9, [((rank, cols), jnp.bfloat16)], 1)[0]
        partial = swap(partial.reshape(n_dp * n_tensor, rows // (n_dp * n_tensor), rank), BOTH)
        left = share(jnp.sum(partial, axis=0), BOTH).reshape(rows, rank)
    with jax.named_scope("totals"):
        totals = [total] + [lax.ppermute(total, "dp", turn(k)) for k in range(1, n_dp)]
    with jax.named_scope("products"):
        prod_rows = rank * cols // EDGE // 2
        keep, send = call(
            functools.partial(products, n_near, n_far),
            [(prod_rows + slot, EDGE)] * 2,
            (place, core, left, total),
            10**9,
            [(2, prod_rows + slot, EDGE), (n_slots * slot, EDGE)],
            2,
        )
        both = keep + other_core(send)
        for axis, n in (("near", n_near), ("far", n_far)):
            prod_rows = both.shape[0] - slot
            prod = both[:prod_rows].reshape(n, prod_rows // n, EDGE)
            gram = jnp.broadcast_to(both[prod_rows:][None], (n, slot, EDGE))
            both = swap(jnp.concatenate([prod, gram], axis=1), axis)
            if axis == "near":
                both, totals[1], totals[3] = lax.optimization_barrier((both, totals[1], totals[3]))
            else:
                both, totals[2] = lax.optimization_barrier((both, totals[2]))
            both = jnp.sum(both, axis=0)
        prod, gram = both[:-slot], both[-slot:]
        gram = share(gram, BOTH)
        prod, gram = lax.optimization_barrier((prod, gram))
    with jax.named_scope("factor"):
        half = (rank // 2, rank)
        top = call(
            factor_top,
            [(3 * EDGE, rank)],
            (core, gram, other_core(gram)),
            10**10,
            [(n_slots * slot, EDGE)],
            1,
        )[0]
        prod = share(prod, "far")
        prod, top = lax.optimization_barrier((prod, top))
        low, left_basis = call(factor_rest, [half, (rows, rank)], (top, left), 10**10)
        prod = share(prod, "near")
        prod, low = lax.optimization_barrier((prod, low))
    with jax.named_scope("right"):
        prod = prod.reshape(n_fsdp // 2, cols // EDGE, rank_local, EDGE)
        right_t, squares = call(
            finish,
            [(rank, cols), (8, rank)],
            (core, prod, other_core(prod), top, low),
            2 * 10**9,
            [(rank, cols)],
            1,
        )
    with jax.named_scope("norms"):
        squares = share(squares[:1], BOTH).reshape(n_dp * n_tensor, rank)
    with jax.named_scope("outputs"):
        mixed = call(
            functools.partial(outputs, factor_scale),
            [(n_dp, 2 * rows + rank_local, cols)],
            (me, squares, left_basis, right_t),
            10**9,
            (),
            1,
            jnp.bfloat16,
        )[0]
        mixed = swap(mixed, "dp")
        new_momentum, update, basis = call(
            merge,
            [(rows, local_cols), (rows, local_cols), (rank_local, local_cols)],
            (d.reshape(1), mixed, *totals),
            10**6,
            (),
            1,
            (jnp.float32, jnp.bfloat16, jnp.bfloat16),
        )
    return (new_momentum, update, basis.T)


def solution(mesh):
    n_dp, n_fsdp, n_tensor = (mesh.shape[a] for a in ("dp", "fsdp", "tensor"))
    near = 4
    far = n_fsdp // 2 // near
    fine = Mesh(mesh.devices.reshape(n_dp, far, near, 2, n_tensor), ("dp", "far", "near", "core", "tensor"))
    fsdp = ("far", "near", "core")
    in_specs = (P(fsdp, "tensor"), P("dp", fsdp, "tensor"), P("tensor", fsdp))
    out_specs = (P(fsdp, "tensor"), P(fsdp, "tensor"), P("tensor", fsdp))
    return jax.shard_map(
        per_device, mesh=fine, in_specs=in_specs, out_specs=out_specs, check_vma=False
    )
```

```python
import functools
import math

import jax
import jax.numpy as jnp
from jax import lax
from jax.experimental import pallas as pl
from jax.experimental.pallas import tpu as pltpu
from jax.sharding import Mesh
from jax.sharding import PartitionSpec as P

HIGH = lax.Precision.HIGHEST
EDGE = 128
BOTH = ("dp", "tensor")
VMEM = pl.BlockSpec(memory_space=pltpu.VMEM)
SMEM = pl.BlockSpec(memory_space=pltpu.SMEM)


def dot(a, b, dims):
    return lax.dot_general(a, b, (dims, ((), ())), precision=HIGH, preferred_element_type=jnp.float32)


def call(kernel, shapes, args, flops, scratch=(), scalars=0, dtype=jnp.float32):
    dtypes = dtype if isinstance(dtype, tuple) else (dtype,) * len(shapes)
    return pl.pallas_call(
        kernel,
        out_shape=[jax.ShapeDtypeStruct(s, t) for s, t in zip(shapes, dtypes)],
        in_specs=[SMEM] * scalars + [VMEM] * (len(args) - scalars),
        out_specs=[VMEM] * len(shapes),
        scratch_shapes=[
            pltpu.VMEM(*s) if isinstance(s[-1], type) else pltpu.VMEM(s, jnp.float32) for s in scratch
        ],
        compiler_params=pltpu.CompilerParams(vmem_limit_bytes=32 * 1024 * 1024),
        cost_estimate=pl.CostEstimate(flops=flops, bytes_accessed=4 * 1024 * 1024, transcendentals=0),
        name=kernel.func.__name__ if isinstance(kernel, functools.partial) else kernel.__name__,
    )(*args)


def invert_block(block):
    size = block.shape[0]
    steps = size // 8
    sub = lax.broadcasted_iota(jnp.int32, (8, size), 0)
    lane = lax.broadcasted_iota(jnp.int32, (8, size), 1)
    full = (8, size)
    rows = [block[8 * i : 8 * i + 8] for i in range(steps)]
    done = []
    for k in range(steps):
        here = (lane >= 8 * k) & (lane < 8 * k + 8)
        columns = [[jnp.broadcast_to(r[:, 8 * k + m : 8 * k + m + 1], full) for m in range(8)] for r in rows[k:]]
        cur = jnp.where(here, (lane - 8 * k == sub).astype(jnp.float32), rows[k])
        col = columns[0]
        result = jnp.zeros(full, jnp.float32)
        for j in range(8):
            at = sub == j
            pivot = jnp.broadcast_to(col[j][j : j + 1], full)
            row = jnp.broadcast_to(cur[j : j + 1], full)
            result = jnp.where(at, row * lax.rsqrt(pivot), result)
            recip = 1.0 / pivot
            mult = jnp.where(at, -1.0, col[j])
            cur = jnp.where(at, 0.0, cur) - (mult * row) * recip
            for m in range(j + 1, 8):
                lead = jnp.broadcast_to(col[m][j : j + 1], full)
                col[m] = jnp.where(at, 0.0, col[m]) - (mult * lead) * recip
        done.append(jnp.where(lane <= 8 * k + sub, result, 0.0))
        if k + 1 < steps:
            spread = [jnp.broadcast_to(cur[m : m + 1], full) for m in range(8)]
            for i in range(k + 1, steps):
                acc = jnp.where(here, 0.0, rows[i])
                for m in range(8):
                    acc = acc - columns[i - k][m] * spread[m]
                rows[i] = acc
    return jnp.concatenate(done, axis=0)


def upper_blocks(count):
    return [(k, j) for k in range(count) for j in range(k, count)]


def factor_top(core_ref, own_ref, other_ref, top_ref, gram):
    slot = own_ref.shape[1]
    for refs, core in ((own_ref, core_ref[0]), (other_ref, 1 - core_ref[0])):
        for j in range(refs.shape[0]):
            gram[pl.ds(pl.multiple_of((2 * j + core) * slot, 8), slot), :] = refs[j]
    g00, g01, g02, g03, g11, g12, g13, g22, g23, g33 = (
        gram[at * EDGE : (at + 1) * EDGE, :] for at in range(len(upper_blocks(4)))
    )
    e1, e2, e3 = EDGE, 2 * EDGE, 3 * EDGE
    inv = invert_block(g00)
    upper = dot(inv, jnp.concatenate([g01, g02, g03], axis=1), ((1,), (0,)))
    top_ref[:e1, :e1] = inv
    top_ref[:e1, e1:e2] = jnp.zeros((e1, e1), jnp.float32)
    top_ref[:e1, e2:] = upper[:, e1:]
    less = dot(upper[:, :e1], jnp.concatenate([inv, upper], axis=1), ((0,), (0,)))
    inv = invert_block(g11 - less[:, e1:e2])
    top_ref[e1:e2, :e1] = dot(inv, -less[:, :e1], ((1,), (0,)))
    top_ref[e1:e2, e1:e2] = inv
    top_ref[e1:e2, e2:] = dot(inv, jnp.concatenate([g12, g13], axis=1) - less[:, e2:], ((1,), (0,)))
    top_ref[e2:, :] = jnp.concatenate([g22, g23, g33, jnp.zeros_like(g33)], axis=1)


def factor_rest(top_ref, left_ref, low_ref, basis_ref):
    e1, e2, e3 = EDGE, 2 * EDGE, 3 * EDGE
    less = dot(top_ref[:e2, e2:], top_ref[:e2, :], ((0,), (0,)))
    inv = invert_block(top_ref[e2:, :e1] - less[:e1, e2:e3])
    upper = dot(inv, top_ref[e2:, e1:e2] - less[:e1, e3:], ((1,), (0,)))
    row = dot(inv, -less[:e1, :e2], ((1,), (0,)))
    low_ref[:e1, :e2] = row
    low_ref[:e1, e2:e3] = inv
    low_ref[:e1, e3:] = jnp.zeros((e1, e1), jnp.float32)
    last = dot(upper, jnp.concatenate([row, inv, upper], axis=1), ((0,), (0,)))
    inv = invert_block(top_ref[e2:, e2:e3] - less[e1:, e3:] - last[:, e3:])
    row = jnp.concatenate([-less[e1:, :e2] - last[:, :e2], -last[:, e2:e3]], axis=1)
    low_ref[e1:, :e3] = dot(inv, row, ((1,), (0,)))
    low_ref[e1:, e3:] = inv
    basis_ref[:, :e2] = dot(left_ref[:, :e2], top_ref[:e2, :e2], ((1,), (1,)))
    basis_ref[:, e2:] = dot(left_ref[...], low_ref[...], ((1,), (1,)))


def left_part(core_ref, own_ref, other_ref, momentum_ref, *refs):
    grads, (out_ref, total_ref, basis) = refs[:-3], refs[-3:]
    summed = grads[0][...].astype(jnp.float32)
    for ref in grads[1:]:
        summed += ref[...].astype(jnp.float32)
    total_ref[...] = momentum_ref[...] + summed
    count, ranks, _ = own_ref.shape
    for refs, core in ((own_ref, core_ref[0]), (other_ref, 1 - core_ref[0])):
        for z in range(count):
            basis[pl.ds(pl.multiple_of((2 * z + core) * ranks, ranks), ranks), :] = refs[z]
    rest = total_ref[...]
    left = jnp.zeros(out_ref.shape, jnp.float32)
    for _ in range(3):
        part = rest.astype(jnp.bfloat16)
        left += lax.dot_general(part, basis[...], (((1,), (1,)), ((), ())), preferred_element_type=jnp.float32)
        rest -= part.astype(jnp.float32)
    out_ref[...] = left


def products(near, far, place_ref, core_ref, left_ref, total_ref, keep_ref, send_ref, out, gram):
    left = left_ref[...]
    rank = left.shape[1]
    cols = total_ref.shape[1]
    blocks = cols // EDGE
    piece = rank // (2 * near * far)
    prod = dot(left, total_ref[...], ((0,), (0,)))
    for i in range(2 * near * far):
        to, rest = divmod(i, near * far)
        for j in range(blocks):
            at = (rest * blocks + j) * piece
            out[to, at : at + piece, :] = prod[i * piece : (i + 1) * piece, j * EDGE : (j + 1) * EDGE]
    at = 0
    for k in range(rank // EDGE):
        row = dot(left[:, k * EDGE : (k + 1) * EDGE], left[:, k * EDGE :], ((0,), (0,)))
        for j in range(row.shape[1] // EDGE):
            gram[at : at + EDGE, :] = row[:, j * EDGE : (j + 1) * EDGE]
            at += EDGE
    begin = near * far * blocks * piece
    slot = out.shape[1] - begin
    for to in range(2):
        out[to, begin:, :] = gram[pl.ds(pl.multiple_of((2 * place_ref[0] + to) * slot, 8), slot), :]
    keep_ref[...] = out[core_ref[0]]
    send_ref[...] = out[1 - core_ref[0]]


def finish(core_ref, own_ref, other_ref, top_ref, low_ref, right_ref, squares_ref, prod):
    half = low_ref.shape[0]
    for refs, core in ((own_ref, core_ref[0]), (other_ref, 1 - core_ref[0])):
        at = pl.ds(pl.multiple_of(core * half, half), half)
        for j in range(refs.shape[1]):
            prod[at, j * EDGE : (j + 1) * EDGE] = refs[:, j].reshape(half, EDGE)
    top = dot(top_ref[:half, :half], prod[:half, :], ((1,), (0,)))
    low = dot(low_ref[...], prod[...], ((1,), (0,)))
    right_ref[:half, :] = top
    right_ref[half:, :] = low
    ones = jnp.ones((8, prod.shape[1]), jnp.float32)
    squares_ref[:, :half] = dot(ones, top * top, ((1,), (1,)))
    squares_ref[:, half:] = dot(ones, low * low, ((1,), (1,)))


def outputs(scale, me_ref, squares_ref, basis_ref, right_ref, out_ref):
    rows, rank = basis_ref.shape
    own = out_ref.shape[1] - 2 * rows
    norms = lax.rsqrt(jnp.sum(squares_ref[...], axis=0, keepdims=True) + 1e-06)
    basis = basis_ref[...]
    row = lax.broadcasted_iota(jnp.int32, (own, rank), 0)
    lane = lax.broadcasted_iota(jnp.int32, (own, rank), 1)
    pick = jnp.where(lane == row + me_ref[0] * own, norms, 0.0)
    mixed = dot(jnp.concatenate([0.05 * basis, basis * (scale * norms), pick], axis=0), right_ref[...], ((1,), (0,)))
    mixed = mixed.astype(out_ref.dtype)
    for to in range(out_ref.shape[0]):
        out_ref[to] = mixed


def merge(d_ref, mixed_ref, *refs):
    totals, (momentum_ref, update_ref, basis_ref) = refs[:-3], refs[-3:]
    n = len(totals)
    rows, cols = totals[0].shape
    for k in range(n):
        q = lax.rem(d_ref[0] + (n - k), n)
        at = pl.ds(pl.multiple_of(q * cols, cols), cols)
        momentum_ref[:, at] = totals[k][...] - mixed_ref[q, :rows, :].astype(jnp.float32)
    for q in range(n):
        update_ref[:, q * cols : (q + 1) * cols] = mixed_ref[q, rows : 2 * rows, :]
        basis_ref[:, q * cols : (q + 1) * cols] = mixed_ref[q, 2 * rows :, :]


def swap(x, axis):
    return lax.all_to_all(x, axis, 0, 0, tiled=True)


def share(x, axis):
    return swap(jnp.broadcast_to(x[None], (lax.axis_size(axis),) + x.shape), axis)


def other_core(x):
    return lax.ppermute(x, "core", [(0, 1), (1, 0)])


def per_device(momentum, grads, right_basis):
    rows, local_cols = momentum.shape
    n_dp, n_far, n_near, n_tensor = (lax.axis_size(a) for a in ("dp", "far", "near", "tensor"))
    n_slots = 2 * n_dp * n_tensor
    rank_local = right_basis.shape[1]
    n_fsdp = 2 * n_far * n_near
    rank = rank_local * n_fsdp
    cols = local_cols // n_dp
    factor_scale = math.sqrt(rows * n_fsdp * local_cols * n_tensor / rank)
    d = lax.axis_index("dp")
    me = lax.axis_index(("far", "near", "core")).reshape(1)
    place = lax.axis_index(BOTH).reshape(1)
    core = lax.axis_index("core").reshape(1)
    slot = len(upper_blocks(rank // EDGE)) * EDGE // n_slots

    def turn(k):
        return [(i, (i + k) % n_dp) for i in range(n_dp)]

    with jax.named_scope("basis"):
        mine = lax.dynamic_slice_in_dim(right_basis.T, d * cols, cols, 1)
        part = share(mine, ("far", "near"))
    with jax.named_scope("total"):
        def column(x, k):
            return lax.dynamic_slice_in_dim(x, (d + k) % n_dp * cols, cols, 1)

        blocks = [lax.ppermute(column(grads[0], k), "dp", turn(k)) for k in range(1, n_dp)]
        part, *blocks = lax.optimization_barrier((part, *blocks, column(momentum, 0)))
        other = other_core(part)
    with jax.named_scope("left"):
        partial, total = call(
            left_part,
            [(rows, rank), (rows, cols)],
            (core, part, other, blocks[-1], column(grads[0], 0), *blocks[:-1]),
            10**9,
            [((rank, cols), jnp.bfloat16)],
            1,
        )
        partial = swap(partial.reshape(n_dp * n_tensor, rows // (n_dp * n_tensor), rank), BOTH)
        left = share(jnp.sum(partial, axis=0), BOTH).reshape(rows, rank)
    with jax.named_scope("totals"):
        totals = [total] + [lax.ppermute(total, "dp", turn(k)) for k in range(1, n_dp)]
    with jax.named_scope("products"):
        prod_rows = rank * cols // EDGE // 2
        keep, send = call(
            functools.partial(products, n_near, n_far),
            [(prod_rows + slot, EDGE)] * 2,
            (place, core, left, total),
            10**9,
            [(2, prod_rows + slot, EDGE), (n_slots * slot, EDGE)],
            2,
        )
        both = keep + other_core(send)
        for axis, n in (("near", n_near), ("far", n_far)):
            prod_rows = both.shape[0] - slot
            prod = both[:prod_rows].reshape(n, prod_rows // n, EDGE)
            gram = jnp.broadcast_to(both[prod_rows:][None], (n, slot, EDGE))
            both = swap(jnp.concatenate([prod, gram], axis=1), axis)
            if axis == "near":
                both, totals[1], totals[3] = lax.optimization_barrier((both, totals[1], totals[3]))
            else:
                both, totals[2] = lax.optimization_barrier((both, totals[2]))
            both = jnp.sum(both, axis=0)
        prod, gram = both[:-slot], both[-slot:]
        gram = share(gram, BOTH)
        prod, gram = lax.optimization_barrier((prod, gram))
    with jax.named_scope("factor"):
        half = (rank // 2, rank)
        top = call(
            factor_top,
            [(3 * EDGE, rank)],
            (core, gram, other_core(gram)),
            10**10,
            [(n_slots * slot, EDGE)],
            1,
        )[0]
        prod = share(prod, "far")
        prod, top = lax.optimization_barrier((prod, top))
        low, left_basis = call(factor_rest, [half, (rows, rank)], (top, left), 10**10)
        prod = share(prod, "near")
        prod, low = lax.optimization_barrier((prod, low))
    with jax.named_scope("right"):
        prod = prod.reshape(n_fsdp // 2, cols // EDGE, rank_local, EDGE)
        right_t, squares = call(
            finish,
            [(rank, cols), (8, rank)],
            (core, prod, other_core(prod), top, low),
            2 * 10**9,
            [(rank, cols)],
            1,
        )
    with jax.named_scope("norms"):
        squares = share(squares[:1], BOTH).reshape(n_dp * n_tensor, rank)
    with jax.named_scope("outputs"):
        mixed = call(
            functools.partial(outputs, factor_scale),
            [(n_dp, 2 * rows + rank_local, cols)],
            (me, squares, left_basis, right_t),
            10**9,
            (),
            1,
            jnp.bfloat16,
        )[0]
        mixed = swap(mixed, "dp")
        new_momentum, update, basis = call(
            merge,
            [(rows, local_cols), (rows, local_cols), (rank_local, local_cols)],
            (d.reshape(1), mixed, *totals),
            10**6,
            (),
            1,
            (jnp.float32, jnp.bfloat16, jnp.bfloat16),
        )
    return (new_momentum, update, basis.T)


def solution(mesh):
    n_dp, n_fsdp, n_tensor = (mesh.shape[a] for a in ("dp", "fsdp", "tensor"))
    near = 4
    far = n_fsdp // 2 // near
    fine = Mesh(mesh.devices.reshape(n_dp, far, near, 2, n_tensor), ("dp", "far", "near", "core", "tensor"))
    fsdp = ("far", "near", "core")
    in_specs = (P(fsdp, "tensor"), P("dp", fsdp, "tensor"), P("tensor", fsdp))
    out_specs = (P(fsdp, "tensor"), P(fsdp, "tensor"), P("tensor", fsdp))
    return jax.shard_map(
        per_device, mesh=fine, in_specs=in_specs, out_specs=out_specs, check_vma=False
    )
```
